256 devices in a mesh: space: 64 (over y, x_lo, z), chan: 4 (over x_hi, core).
Axes of the slice: x: 4 (x_hi: 2, x_lo: 2; x = x_hi * 2 + x_lo), y: 4, z: 8, core: 2. Of those that a mesh axis runs over, the one named last changes fastest.
Arguments:
- cotangent: bfloat16 [64, 768, 896], P('space', 'chan'), may hold values from -6 to 6
- active_first: bfloat16 [64, 768, 896], P('space', 'chan'), may hold values from -16 to 16
- active_second: bfloat16 [64, 768, 896], P('space', 'chan'), may hold values from -16 to 16
- spatial_first: bfloat16 [3, 3, 768, 768], P(None, None, 'chan'), may hold values from -0.078125 to 0.078125
- spatial_second: bfloat16 [3, 3, 768, 768], P(None, None, 'chan'), may hold values from -0.078125 to 0.078125
- temporal_first: bfloat16 [7, 768, 768], P(None, 'chan'), may hold values from -0.078125 to 0.078125
- temporal_second: bfloat16 [7, 768, 768], P(None, 'chan'), may hold values from -0.078125 to 0.078125
Outputs:
- input_grad: bfloat16 [64, 768, 896], P('space', 'chan')
- filter_first: float32 [7, 768, 768], P(None, 'space', 'chan')
- filter_second: float32 [7, 768, 768], P(None, 'space', 'chan')
The draws below stay inside these ranges and needn't reach their ends.
All inputs are finite; a program needn't handle non-finite values.
Results may differ from the reference program's by a relative error of at most 0.022.
Values may be sent and summed in bfloat16 or wider, within the bound.
No kernel may reach another device: no remote copies, remote signals or barrier semaphores. Data moves between devices by JAX's collectives and lax.ppermute only.
A program may use at most 128 MiB of HBM per device.

```python
import math
import jax
import jax.numpy as jnp
from jax import lax

C = 768
TAPS = 7
HGT = 16
WID = 28
CLIPS = 2
FRAMES = 64
CELLS = 896
N_CHAN = 4


def spiked(entries, key, source, target, shards_of, factor):
    owner, partner = [(jnp.arange(entries.shape[dim]) // (entries.shape[dim] // shards_of)).reshape([-1 if axis == dim else 1 for axis in range(entries.ndim)]) for dim in (source, target)]
    chosen = jax.random.permutation(key, shards_of)[partner]
    strong = (owner == chosen) | (owner == (partner + shards_of // 2) % shards_of)
    return jnp.where(strong, factor * entries, entries)


def block_levels(rng, extent, pieces, smallest, high):
    level = 1.0
    for axis_at, blocks in pieces:
        draws = jax.random.uniform(jax.random.fold_in(jax.random.fold_in(rng, 6), axis_at), (blocks,), jnp.float32, smallest / len(pieces), high / len(pieces))
        level = level * jnp.repeat(jnp.exp(draws), extent[axis_at] // blocks).reshape((-1,) + (1,) * (len(extent) - 1 - axis_at))
    return level


def centred(rng, dims, width, limit, pieces=(), kind=jnp.bfloat16):
    array = jax.random.normal(rng, dims, jnp.float32) * width
    if len(pieces) > 0:
        array = block_levels(rng, dims, pieces, -0.22, 0.18) * array
    return jnp.clip(array, min=-limit, max=limit).astype(kind)


def heavy_noise(rng, dims, spread, bound, shards, heavy, kind=jnp.bfloat16):
    values = spread * jax.random.normal(rng, dims, jnp.float32)
    if shards:
        values = values * block_levels(rng, dims, shards, -0.22, 0.18)
    return jnp.clip(spiked(values, jax.random.fold_in(rng, 3), *heavy), -bound, bound).astype(kind)


def setup_inputs(seed: int = 0) -> dict:
    splits = jax.random.split(jax.random.key(seed), 8)
    return {
        "cotangent": centred(splits[0], (FRAMES, C, CELLS), 1.0, 6.0, ((0, 64), (1, 4))),
        "active_first": heavy_noise(splits[1], (FRAMES, C, CELLS), 1.0, 16.0, ((0, 64), (1, 4)), (0, 1, 64, 4.0)),
        "active_second": heavy_noise(splits[2], (FRAMES, C, CELLS), 1.0, 16.0, ((0, 64), (1, 4)), (0, 1, 64, 4.0)),
        "spatial_first": centred(splits[3], (3, 3, C, C), (9 * C) ** -0.5, 0.078125, ((2, 4),)),
        "spatial_second": centred(splits[4], (3, 3, C, C), (9 * C) ** -0.5, 0.078125, ((2, 4),)),
        "temporal_first": centred(splits[5], (TAPS, C, C), (TAPS * C) ** -0.5, 0.078125, ((1, 4),)),
        "temporal_second": centred(splits[6], (TAPS, C, C), (TAPS * C) ** -0.5, 0.078125, ((1, 4),)),
    }


def temporal_back(upstream, hidden, weights):
    frames = upstream.shape[0]
    channels = upstream.shape[3]
    portion = channels // N_CHAN
    half_taps = TAPS // 2
    widths = ((half_taps, half_taps), (0, 0), (0, 0), (0, 0))
    grad_pad = jnp.pad(upstream.astype(jnp.float32), widths)
    hidden_pad = jnp.pad(hidden.astype(jnp.float32), widths)
    full_weights = weights.astype(jnp.float32)

    def add_group(running, group):
        grad_part = lax.dynamic_slice_in_dim(grad_pad, group * portion, portion, 3)
        weight_part = lax.dynamic_slice_in_dim(full_weights, group * portion, portion, 2)
        contrib = jnp.zeros(upstream.shape[:3] + (channels,), jnp.float32)
        for tap in range(TAPS):
            start = 2 * half_taps - tap
            contrib = contrib + jnp.einsum('fpqc,dc->fpqd', grad_part[start:start + frames], weight_part[tap])
        rounded = lax.optimization_barrier(contrib.astype(jnp.bfloat16))
        return (running + rounded.astype(jnp.float32), None)
    zeros = jnp.zeros(upstream.shape[:3] + (channels,), jnp.float32)
    running, unused = lax.scan(add_group, zeros, jnp.arange(N_CHAN, dtype=jnp.int32))
    own_grad = upstream.astype(jnp.float32)
    filters = jnp.stack([jnp.einsum('fpqd,fpqc->dc', hidden_pad[tap:tap + frames], own_grad) for tap in range(TAPS)])
    return (running.astype(jnp.bfloat16), filters)

def spatial_back(masked, weights):
    channels = masked.shape[3]
    portion = channels // N_CHAN
    grid = masked.reshape(masked.shape[0] * masked.shape[1], HGT, WID, channels).astype(jnp.float32)
    padded = jnp.pad(grid, ((0, 0), (1, 1), (1, 1), (0, 0)))
    full_weights = weights.astype(jnp.float32)

    def add_group(running, group):
        grad_part = lax.dynamic_slice_in_dim(padded, group * portion, portion, 3)
        weight_part = lax.dynamic_slice_in_dim(full_weights, group * portion, portion, 3)
        contrib = jnp.zeros(grid.shape, jnp.float32)
        for row in range(3):
            for col in range(3):
                window = grad_part[:, 2 - row:2 - row + HGT, 2 - col:2 - col + WID]
                contrib = contrib + jnp.einsum('nyxc,dc->nyxd', window, weight_part[row, col])
        rounded = lax.optimization_barrier(contrib.astype(jnp.bfloat16))
        return (running + rounded.astype(jnp.float32), None)
    running, unused = lax.scan(add_group, jnp.zeros(grid.shape, jnp.float32), jnp.arange(N_CHAN, dtype=jnp.int32))
    return running.reshape(masked.shape)

def backward_block(upstream, active, spatial_weights, temporal_weights):
    hidden = jnp.maximum(active, jnp.zeros((), jnp.bfloat16))
    back, filters = temporal_back(upstream, hidden, temporal_weights)
    masked = jnp.where(active > 0, back, jnp.zeros_like(back))
    summed = spatial_back(masked, spatial_weights)
    result = (upstream.astype(jnp.float32) + summed).astype(jnp.bfloat16)
    return (result, filters)

def to_inner(field):
    frames, channels = (field.shape[0], field.shape[1])
    return field.reshape(frames, channels, CLIPS, HGT * WID).transpose(0, 2, 3, 1)

def to_outer(field):
    frames, channels = (field.shape[0], field.shape[3])
    return field.transpose(0, 3, 1, 2).reshape(frames, channels, CLIPS * HGT * WID)

def reference(cotangent, active_first, active_second, spatial_first, spatial_second, temporal_first, temporal_second):
    factor = 1.0 / math.sqrt(FRAMES * CLIPS * HGT * WID)
    middle, filters_second = backward_block(to_inner(cotangent), to_inner(active_second), spatial_second.transpose(0, 1, 3, 2), temporal_second.transpose(0, 2, 1))
    input_grad, filters_first = backward_block(middle, to_inner(active_first), spatial_first.transpose(0, 1, 3, 2), temporal_first.transpose(0, 2, 1))
    return (to_outer(input_grad), filters_first * factor, filters_second * factor)
```

```python
import functools
import math

import jax
import jax.numpy as jnp
from jax import lax
from jax.experimental import pallas as pl
from jax.experimental.pallas import tpu as pltpu
from jax.sharding import Mesh
from jax.sharding import PartitionSpec as P

TAPS = 7
HGT = 16
WID = 28
CLIPS = 2
PEERS = 64
CH = 192
CHANS = 4
FULL = CH * CHANS
CELLS = CLIPS * HGT * WID
OWN = FULL // PEERS
PER = 8
ORDER = (0, 6, 1, 2, 3, 4, 5)
FAR = 2 * CH
STACK = TAPS * CH
LOW = 1408
FLANES = LOW + 4 * CH
SPACE = ("y", "xl", "z")
F32 = jnp.float32
BF16 = jnp.bfloat16
NT = (((1,), (1,)), ((), ()))
VMEM = 24 * 1024 * 1024


def params():
    return pltpu.CompilerParams(vmem_limit_bytes=VMEM)


def cost(flops, moved):
    return pl.CostEstimate(flops=int(flops), bytes_accessed=int(moved), transcendentals=0)


def whole(shape):
    return pl.BlockSpec(shape, lambda i, *_: (0,) * len(shape))


def call(kernel, name, scalars, ins, outs, scratch=(), steps=1, in_specs=None, out_specs=None, flops=0, after=()):
    moved = sum(math.prod(x.shape) * x.dtype.itemsize for x in list(ins) + list(outs))
    n, m = 1 + len(ins), len(after)

    def body(*refs):
        kernel(*refs[:n], *refs[n + m :])

    return pl.pallas_call(
        body,
        grid_spec=pltpu.PrefetchScalarGridSpec(
            num_scalar_prefetch=1,
            grid=(steps,),
            in_specs=(in_specs or [whole(x.shape) for x in ins]) + [pl.BlockSpec(memory_space=pl.ANY)] * m,
            out_specs=out_specs or [whole(x.shape) for x in outs],
            scratch_shapes=list(scratch),
        ),
        out_shape=list(outs),
        compiler_params=params(),
        cost_estimate=cost(flops, moved),
        name=name,
    )(scalars, *ins, *after)


def like(shape, dtype=BF16):
    return jax.ShapeDtypeStruct(shape, dtype)


def turn_kernel(taps, place_ref, w_ref, out_ref):
    row = lax.broadcasted_iota(jnp.int32, (FULL, 1), 0)
    want = row + (place_ref[0]) * CH
    for slot in range(1, CHANS):
        want = jnp.where(row >= slot * CH, row + (place_ref[slot] - slot) * CH, want)
    lane = lax.broadcasted_iota(jnp.int32, (FULL, FULL), 1)
    pick = jnp.where(lane == want, 1.0, 0.0).astype(BF16)
    for n in range(0, len(taps), 2):
        pair = [lax.dot_general(pick, w_ref[tap], NT, preferred_element_type=F32) for tap in taps[n : n + 2]]
        pair = pair[0] if len(pair) == 1 else jnp.concatenate(pair, axis=1)
        out_ref[:, n * CH : n * CH + pair.shape[1]] = pair.astype(BF16)


def turn(place, w, taps, after=()):
    return call(
        functools.partial(turn_kernel, taps),
        "turn",
        place,
        [w],
        [like((FULL, len(taps) * CH))],
        flops=2 * FULL * FULL * CH * len(taps),
        after=after,
    )[0]


def arrange_kernel(place_ref, a_ref, b_ref, c_ref, d_ref, out_ref):
    step = pl.program_id(0)
    half = PEERS // F_STEPS * PER
    row = lax.broadcasted_iota(jnp.int32, (2 * half, 1), 0)
    low = row < half
    at = jnp.where(low, row, row - half)
    place = step * (PEERS // F_STEPS) + lax.shift_right_logical(at, 3)
    peer = lax.bitwise_and(place, 7) * 8 + lax.shift_right_logical(place, 3)
    inner = jnp.where(low, lax.bitwise_and(at, 7), 8 + lax.bitwise_and(at, 3))
    want = peer * OWN + inner
    lane = lax.broadcasted_iota(jnp.int32, (2 * half, CH), 1)
    total = None
    for slot, ref in enumerate((a_ref, b_ref, c_ref, d_ref)):
        pick = jnp.where(lane + place_ref[slot] * CH == want, 1.0, 0.0).astype(BF16)
        t = jnp.dot(pick, ref[...], preferred_element_type=F32)
        total = t if total is None else total + t
    out_ref[...] = total.astype(BF16)


F_STEPS = 4
ROWS = 2 * PEERS * PER


def arrange(place, pieces, after=()):
    return call(
        arrange_kernel,
        "arrange",
        place,
        pieces,
        [like((ROWS, CELLS))],
        steps=F_STEPS,
        out_specs=[pl.BlockSpec((ROWS // F_STEPS, CELLS), lambda i, *_: (i, 0))],
        flops=2 * ROWS * FULL * CELLS,
        after=after,
    )[0]


def near_kernel(place_ref, w_ref, a_ref, b_ref, c_ref, d_ref, e_ref, out_ref, stack_ref):
    step = pl.program_id(0)

    @pl.when(step == 0)
    def _():
        for n, ref in enumerate((a_ref, b_ref, c_ref, d_ref, e_ref)):
            stack_ref[n * CH : (n + 1) * CH] = ref[...]

    out_ref[...] = jnp.dot(w_ref[:, FAR:], stack_ref[...], preferred_element_type=F32)


T_STEPS = 4


def temporal_near(place, w, frames, after=()):
    rows = FULL // T_STEPS
    return call(
        near_kernel,
        "temporal_near",
        place,
        [w] + frames,
        [like((FULL, CELLS), F32)],
        scratch=[pltpu.VMEM((5 * CH, CELLS), BF16)],
        steps=T_STEPS,
        in_specs=[pl.BlockSpec((rows, STACK), lambda i, *_: (i, 0))] + [whole((CH, CELLS))] * 5,
        out_specs=[pl.BlockSpec((rows, CELLS), lambda i, *_: (i, 0))],
        flops=2 * FULL * 5 * CH * CELLS,
        after=after,
    )[0]


def far_kernel(place_ref, w_ref, acc_ref, a_ref, b_ref, send_ref, keep_ref, stack_ref):
    step = pl.program_id(0)

    @pl.when(step == 0)
    def _():
        stack_ref[0:CH] = a_ref[...]
        stack_ref[CH:] = b_ref[...]

    v = acc_ref[...] + jnp.dot(w_ref[:, :FAR], stack_ref[...], preferred_element_type=F32)
    v = v.astype(BF16)
    for n in range(CHANS):

        @pl.when(step == n)
        def _():
            (send_ref if n < 2 else keep_ref)[n % 2] = v


def temporal_far(place, w, acc, frames, after=()):
    return call(
        far_kernel,
        "temporal_far",
        place,
        [w, acc] + frames,
        [like((2, CH, CELLS))] * 2,
        scratch=[pltpu.VMEM((FAR, CELLS), BF16)],
        steps=CHANS,
        in_specs=[
            pl.BlockSpec((CH, STACK), lambda i, *_: (i, 0)),
            pl.BlockSpec((CH, CELLS), lambda i, *_: (i, 0)),
        ]
        + [whole((CH, CELLS))] * 2,
        flops=2 * FULL * FAR * CELLS,
        after=after,
    )


def spatial_kernel(place_ref, w_ref, active_ref, keep_ref, got_ref, far_ref, send_ref, out_ref, win_ref):
    step = pl.program_id(0)

    @pl.when(step == 0)
    def _():
        pair = (keep_ref[1].astype(F32) + got_ref[1].astype(F32)).astype(BF16).astype(F32)
        back = (pair + far_ref[...].astype(F32)).astype(BF16).astype(F32)
        masked = jnp.where(active_ref[0].astype(F32) > 0, back, 0.0)
        cell = lax.broadcasted_iota(jnp.int32, (1, CELLS), 1)
        cell = jnp.where(cell < HGT * WID, cell, cell - HGT * WID)
        line = lax.shift_right_logical(cell * 2341, 16)
        spot = cell - line * WID
        for row in range(3):
            for col in range(3):
                down, right = 1 - row, 1 - col
                shift = down * WID + right
                v = masked if shift == 0 else pltpu.roll(masked, (-shift) % CELLS, 1)
                if shift != 0:
                    ok = (line + down >= 0) & (line + down < HGT)
                    ok = ok & (spot + right >= 0) & (spot + right < WID)
                    v = jnp.where(ok, v, 0.0)
                n = row * 3 + col
                win_ref[n * CH : (n + 1) * CH] = v.astype(BF16)

    v = jnp.dot(w_ref[...], win_ref[...], preferred_element_type=F32).astype(BF16)
    for n in range(CHANS):

        @pl.when(step == n)
        def _():
            (send_ref if n < 2 else out_ref)[n % 2] = v


def spatial(place, w, active, keep, got, far, after=()):
    return call(
        spatial_kernel,
        "spatial",
        place,
        [w, active, keep, got, far],
        [like((2, CH, CELLS))] * 2,
        scratch=[pltpu.VMEM((9 * CH, CELLS), BF16)],
        steps=CHANS,
        in_specs=[pl.BlockSpec((CH, 9 * CH), lambda i, *_: (i, 0))]
        + [whole(x.shape) for x in (active, keep, got, far)],
        flops=2 * FULL * 9 * CH * CELLS,
        after=after,
    )


def filter_kernel(place_ref, h_ref, *refs):
    frames, out_ref, stack_ref = refs[:TAPS], refs[TAPS], refs[TAPS + 1]
    step = pl.program_id(0)

    @pl.when(step == 0)
    def _():
        for n, ref in enumerate(frames):
            stack_ref[n * CH : (n + 1) * CH] = ref[...]

    acc = lax.dot_general(h_ref[...], stack_ref[...], NT, preferred_element_type=F32)
    half = PEERS // F_STEPS * PER
    low, rest = acc[:half], acc[half:]
    out_ref[:, 0:LOW] = jnp.concatenate([low, jnp.zeros((half, LOW - STACK), F32)], axis=1).astype(BF16)
    upper = lax.bitwise_and(lax.broadcasted_iota(jnp.int32, (half, 4 * CH), 0), 7) < 4
    wide = jnp.concatenate([rest[:, 4 * CH :], jnp.zeros((half, CH), F32)], axis=1)
    out_ref[:, LOW:] = jnp.where(upper, rest[:, : 4 * CH], wide).astype(BF16)


def filter_partial(place, hidden, frames, after=()):
    rows = PEERS * PER // F_STEPS
    return call(
        filter_kernel,
        "filter_partial",
        place,
        [hidden] + frames,
        [like((PEERS * PER, FLANES))],
        scratch=[pltpu.VMEM((STACK, CELLS), BF16)],
        steps=F_STEPS,
        in_specs=[pl.BlockSpec((ROWS // F_STEPS, CELLS), lambda i, *_: (i, 0))]
        + [whole((CH, CELLS))] * TAPS,
        out_specs=[pl.BlockSpec((rows, FLANES), lambda i, *_: (i, 0))],
        flops=2 * ROWS * STACK * CELLS,
        after=after,
    )[0]


def over_z(part):
    part = lax.psum_scatter(part, "z", scatter_dimension=0, tiled=True)
    return part.reshape(8, PER, FLANES)


def filter_sum_kernel(factor, place_ref, in_ref, *outs):
    both = jnp.sum(in_ref[...].astype(F32), axis=0) * factor
    for n, out_ref in enumerate(outs):
        total = both[n * PER : (n + 1) * PER]
        for at, tap in enumerate(ORDER):
            out_ref[tap, 0:PER] = total[:, at * CH : (at + 1) * CH]
            start = LOW + (at % 4) * CH
            part = total[:, start : start + CH]
            out_ref[tap, PER:OWN] = part[0:4] if at < 4 else part[4:8]


def filter_sum(place, factor, x):
    return call(
        functools.partial(filter_sum_kernel, factor),
        "filter_sum",
        place,
        [x],
        [like((TAPS, OWN, CH), F32)] * 2,
    )


def swap(x, axis):
    return lax.ppermute(x, axis, [(0, 1), (1, 0)])


def later(x):
    return lax.ppermute(x, SPACE, [(i + 1, i) for i in range(PEERS - 1)])


def earlier(x):
    return lax.ppermute(x, SPACE, [(i, i + 1) for i in range(PEERS - 1)])


def gather(hidden):
    far = swap(hidden, "xh")
    return [hidden, far, swap(hidden, "core"), swap(far, "core")]


def chan_sum(send, keep):
    got = swap(send, "core")
    pair = (keep[0].astype(F32) + got[0].astype(F32)).astype(BF16)
    return pair, (keep, got, swap(pair, "xh"))


def halo(x):
    down, up = [later(x)], [earlier(x)]
    for _ in range(2):
        down.append(later(down[-1]))
        up.append(earlier(up[-1]))
    return [down[1], down[0], x, up[0], up[1]], [down[2], up[2]]


def shards(cot, active_first, active_second, spatial_first, spatial_second, temporal_first, temporal_second):
    xh, core = lax.axis_index("xh"), lax.axis_index("core")
    chan = lambda a, b: a * 2 + b
    place = jnp.stack(
        [chan(1 - xh, 1 - core), chan(xh, 1 - core), chan(1 - xh, core), chan(xh, core)]
    ).astype(jnp.int32)
    factor = 1.0 / math.sqrt(PEERS * CELLS)
    nine = tuple(range(9))

    def pieces_of(active):
        own, far, near, cross = gather(jnp.maximum(active[0], jnp.zeros((), BF16)))
        return [cross, near, far, own]

    near, far = halo(cot[0])
    pieces_second = pieces_of(active_second)
    pieces_first = pieces_of(active_first)
    w_t = turn(place, temporal_second, ORDER)
    acc = temporal_near(place, w_t, near)
    pair, back = chan_sum(*temporal_far(place, w_t, acc, far))
    w_s = turn(place, spatial_second.reshape(9, CH, FULL), nine)
    hidden = arrange(place, pieces_second, after=[acc])
    part = filter_partial(place, hidden, far + near, after=[pair])
    part_second = over_z(part)
    pair, (keep, got, away) = chan_sum(*spatial(place, w_s, active_second, *back, after=[part]))
    own = (keep[1].astype(F32) + got[1].astype(F32)).astype(BF16).astype(F32)
    middle = (cot[0].astype(F32) + own + away.astype(F32)).astype(BF16)

    near, far = halo(middle)
    w_t = turn(place, temporal_first, ORDER, after=[pair])
    w_s = turn(place, spatial_first.reshape(9, CH, FULL), nine, after=[pair])
    hidden = arrange(place, pieces_first, after=[pair])
    acc = temporal_near(place, w_t, near, after=[hidden])
    part = filter_partial(place, hidden, far + near)
    part_first = over_z(part)
    pair, back = chan_sum(*temporal_far(place, w_t, acc, far, after=[part]))
    pair, (keep, got, away) = chan_sum(*spatial(place, w_s, active_first, *back))
    own = (keep[1].astype(F32) + got[1].astype(F32)).astype(BF16).astype(F32)
    result = (middle.astype(F32) + own + away.astype(F32)).astype(BF16)

    parts = jnp.concatenate([part_first, part_second], axis=1)
    parts = lax.all_to_all(parts, ("y", "xl"), 0, 0, tiled=True)
    filter_first, filter_second = filter_sum(place, factor, parts)
    return result[None], filter_first, filter_second


def solution(mesh):
    fine = Mesh(mesh.devices.reshape(4, 2, 8, 2, 2), SPACE + ("xh", "core"))
    chan = ("xh", "core")
    return jax.shard_map(
        shards,
        mesh=fine,
        in_specs=(
            P(SPACE, chan, None),
            P(SPACE, chan, None),
            P(SPACE, chan, None),
            P(None, None, chan, None),
            P(None, None, chan, None),
            P(None, chan, None),
            P(None, chan, None),
        ),
        out_specs=(P(SPACE, chan, None), P(None, SPACE, chan), P(None, SPACE, chan)),
        check_vma=False,
    )
```

```python
import functools
import math

import jax
import jax.numpy as jnp
from jax import lax
from jax.experimental import pallas as pl
from jax.experimental.pallas import tpu as pltpu
from jax.sharding import Mesh
from jax.sharding import PartitionSpec as P

TAPS = 7
HGT = 16
WID = 28
CLIPS = 2
PEERS = 64
CH = 192
CHANS = 4
FULL = CH * CHANS
CELLS = CLIPS * HGT * WID
OWN = FULL // PEERS
PER = 8
ORDER = (0, 6, 1, 2, 3, 4, 5)
FAR = 2 * CH
STACK = TAPS * CH
LOW = 1408
FLANES = LOW + 4 * CH
SPACE = ("y", "xl", "z")
F32 = jnp.float32
BF16 = jnp.bfloat16
NT = (((1,), (1,)), ((), ()))
MIB = 1024 * 1024


ANY = pl.BlockSpec(memory_space=pl.ANY)


def fetch(sem, pairs):
    copies = [pltpu.make_async_copy(a, b, sem.at[n]) for n, (a, b) in enumerate(pairs)]
    for copy in copies:
        copy.start()
    return copies


def stacked(ref, count):
    return [ref.at[pl.ds(n * CH, CH)] for n in range(count)]


def cost(flops, moved):
    return pl.CostEstimate(flops=int(flops) // 64, bytes_accessed=int(moved) // 64, transcendentals=0)


def whole(shape):
    return pl.BlockSpec(shape, lambda i, *_: (0,) * len(shape))


def call(kernel, name, scalars, ins, outs, scratch=(), steps=1, vmem=10, in_specs=None, out_specs=None, flops=0, after=()):
    moved = sum(math.prod(x.shape) * x.dtype.itemsize for x in list(ins) + list(outs))
    n, m = 1 + len(ins), len(after)

    def body(*refs):
        kernel(*refs[:n], *refs[n + m :])

    return pl.pallas_call(
        body,
        grid_spec=pltpu.PrefetchScalarGridSpec(
            num_scalar_prefetch=1,
            grid=(steps,),
            in_specs=(in_specs or [whole(x.shape) for x in ins]) + [ANY] * m,
            out_specs=out_specs or [whole(x.shape) for x in outs],
            scratch_shapes=list(scratch),
        ),
        out_shape=list(outs),
        compiler_params=pltpu.CompilerParams(vmem_limit_bytes=vmem * MIB),
        cost_estimate=cost(flops, moved),
        name=name,
    )(scalars, *ins, *after)


def tie(arrays, after):
    count, m = len(arrays), len(after)

    def body(*refs):
        pass

    anywhere = pl.BlockSpec(memory_space=pl.ANY)
    return pl.pallas_call(
        body,
        in_specs=[anywhere] * (count + m),
        out_specs=[anywhere] * count,
        out_shape=[like(x.shape, x.dtype) for x in arrays],
        input_output_aliases={i: i for i in range(count)},
        name="tie",
    )(*arrays, *after)


def like(shape, dtype=BF16):
    return jax.ShapeDtypeStruct(shape, dtype)


def turn_kernel(taps, place_ref, w_ref, out_ref):
    row = lax.broadcasted_iota(jnp.int32, (FULL, 1), 0)
    want = row + (place_ref[0]) * CH
    for slot in range(1, CHANS):
        want = jnp.where(row >= slot * CH, row + (place_ref[slot] - slot) * CH, want)
    lane = lax.broadcasted_iota(jnp.int32, (FULL, FULL), 1)
    pick = jnp.where(lane == want, 1.0, 0.0).astype(BF16)
    for n in range(0, len(taps), 2):
        pair = [lax.dot_general(pick, w_ref[tap], NT, preferred_element_type=F32) for tap in taps[n : n + 2]]
        pair = pair[0] if len(pair) == 1 else jnp.concatenate(pair, axis=1)
        out_ref[:, n * CH : n * CH + pair.shape[1]] = pair.astype(BF16)


def turn(place, w, taps, after=()):
    return call(
        functools.partial(turn_kernel, taps),
        "turn",
        place,
        [w],
        [like((FULL, len(taps) * CH))],
        flops=2 * FULL * FULL * CH * len(taps),
        after=after,
        vmem=16,
    )[0]


def arranged(along_y, step, place_ref, pieces):
    half = PEERS // F_STEPS * PER
    row = lax.broadcasted_iota(jnp.int32, (2 * half, 1), 0)
    low = row < half
    at = jnp.where(low, row, row - half)
    spot = lax.shift_right_logical(at, 3)
    if along_y:
        peer = step * 16 + lax.bitwise_and(spot, 1) * 8 + lax.shift_right_logical(spot, 1)
    else:
        peer = lax.bitwise_and(spot, 7) * 8 + step * 2 + lax.shift_right_logical(spot, 3)
    inner = jnp.where(low, lax.bitwise_and(at, 7), 8 + lax.bitwise_and(at, 3))
    want = peer * OWN + inner
    lane = lax.broadcasted_iota(jnp.int32, (2 * half, CH), 1)
    total = None
    for slot, piece in enumerate(pieces):
        pick = jnp.where(lane + place_ref[slot] * CH == want, 1.0, 0.0).astype(BF16)
        t = jnp.dot(pick, piece, preferred_element_type=F32)
        total = t if total is None else total + t
    return total.astype(BF16)


def arrange_kernel(place_ref, a_ref, b_ref, c_ref, d_ref, out_ref):
    pieces = [ref[...] for ref in (a_ref, b_ref, c_ref, d_ref)]
    out_ref[...] = arranged(False, pl.program_id(0), place_ref, pieces)


F_STEPS = 4
ROWS = 2 * PEERS * PER


def arrange(place, pieces, after=()):
    return call(
        arrange_kernel,
        "arrange",
        place,
        pieces,
        [like((ROWS, CELLS))],
        steps=F_STEPS,
        out_specs=[pl.BlockSpec((ROWS // F_STEPS, CELLS), lambda i, *_: (i, 0))],
        flops=2 * ROWS * FULL * CELLS,
        after=after,
    )[0]


def near_kernel(place_ref, w_ref, a_ref, b_ref, c_ref, d_ref, e_ref, out_ref, stack_ref):
    step = pl.program_id(0)

    @pl.when(step == 0)
    def _():
        for n, ref in enumerate((a_ref, b_ref, c_ref, d_ref, e_ref)):
            stack_ref[n * CH : (n + 1) * CH] = ref[...]

    out_ref[...] = jnp.dot(w_ref[:, FAR:], stack_ref[...], preferred_element_type=F32)


T_STEPS = 4


def temporal_near(place, w, frames, after=()):
    rows = FULL // T_STEPS
    return call(
        near_kernel,
        "temporal_near",
        place,
        [w] + frames,
        [like((FULL, CELLS), F32)],
        scratch=[pltpu.VMEM((5 * CH, CELLS), BF16)],
        steps=T_STEPS,
        in_specs=[pl.BlockSpec((rows, STACK), lambda i, *_: (i, 0))] + [whole((CH, CELLS))] * 5,
        out_specs=[pl.BlockSpec((rows, CELLS), lambda i, *_: (i, 0))],
        flops=2 * FULL * 5 * CH * CELLS,
        after=after,
    )[0]


def far_kernel(place_ref, w_ref, acc_ref, a_ref, b_ref, send_ref, keep_ref, stack_ref):
    step = pl.program_id(0)

    @pl.when(step == 0)
    def _():
        stack_ref[0:CH] = a_ref[...]
        stack_ref[CH:] = b_ref[...]

    v = acc_ref[...] + jnp.dot(w_ref[:, :FAR], stack_ref[...], preferred_element_type=F32)
    v = v.astype(BF16)
    for n in range(CHANS):

        @pl.when(step == n)
        def _():
            (send_ref if n < 2 else keep_ref)[n % 2] = v


def temporal_far(place, w, acc, frames, after=()):
    return call(
        far_kernel,
        "temporal_far",
        place,
        [w, acc] + frames,
        [like((2, CH, CELLS))] * 2,
        scratch=[pltpu.VMEM((FAR, CELLS), BF16)],
        steps=CHANS,
        in_specs=[
            pl.BlockSpec((CH, STACK), lambda i, *_: (i, 0)),
            pl.BlockSpec((CH, CELLS), lambda i, *_: (i, 0)),
        ]
        + [whole((CH, CELLS))] * 2,
        flops=2 * FULL * FAR * CELLS,
        after=after,
    )


def spatial_kernel(place_ref, w_ref, active_ref, keep_ref, got_ref, far_ref, send_ref, out_ref, win_ref):
    step = pl.program_id(0)

    @pl.when(step == 0)
    def _():
        pair = (keep_ref[1].astype(F32) + got_ref[1].astype(F32)).astype(BF16).astype(F32)
        back = (pair + far_ref[...].astype(F32)).astype(BF16).astype(F32)
        masked = jnp.where(active_ref[0].astype(F32) > 0, back, 0.0)
        cell = lax.broadcasted_iota(jnp.int32, (1, CELLS), 1)
        cell = jnp.where(cell < HGT * WID, cell, cell - HGT * WID)
        line = lax.shift_right_logical(cell * 2341, 16)
        spot = cell - line * WID
        for row in range(3):
            for col in range(3):
                down, right = 1 - row, 1 - col
                shift = down * WID + right
                v = masked if shift == 0 else pltpu.roll(masked, (-shift) % CELLS, 1)
                if shift != 0:
                    ok = (line + down >= 0) & (line + down < HGT)
                    ok = ok & (spot + right >= 0) & (spot + right < WID)
                    v = jnp.where(ok, v, 0.0)
                n = row * 3 + col
                win_ref[n * CH : (n + 1) * CH] = v.astype(BF16)

    v = jnp.dot(w_ref[...], win_ref[...], preferred_element_type=F32).astype(BF16)
    for n in range(CHANS):

        @pl.when(step == n)
        def _():
            (send_ref if n < 2 else out_ref)[n % 2] = v


def spatial(place, w, active, keep, got, far, after=()):
    return call(
        spatial_kernel,
        "spatial",
        place,
        [w, active, keep, got, far],
        [like((2, CH, CELLS))] * 2,
        scratch=[pltpu.VMEM((9 * CH, CELLS), BF16)],
        steps=CHANS,
        in_specs=[pl.BlockSpec((CH, 9 * CH), lambda i, *_: (i, 0))]
        + [whole(x.shape) for x in (active, keep, got, far)],
        flops=2 * FULL * 9 * CH * CELLS,
        after=after,
        vmem=18,
    )


def partial(hidden, stack_ref, out_ref):
    acc = lax.dot_general(hidden, stack_ref[...], NT, preferred_element_type=F32)
    half = PEERS // F_STEPS * PER
    low, rest = acc[:half], acc[half:]
    out_ref[:, 0:LOW] = jnp.concatenate([low, jnp.zeros((half, LOW - STACK), F32)], axis=1).astype(BF16)
    upper = lax.bitwise_and(lax.broadcasted_iota(jnp.int32, (half, 4 * CH), 0), 7) < 4
    wide = jnp.concatenate([rest[:, 4 * CH :], jnp.zeros((half, CH), F32)], axis=1)
    out_ref[:, LOW:] = jnp.where(upper, rest[:, : 4 * CH], wide).astype(BF16)


PART = like((PEERS * PER, FLANES))


def filter_kernel(place_ref, h_ref, *refs):
    frames, (out_ref, stack_ref) = refs[:TAPS], refs[TAPS:]

    @pl.when(pl.program_id(0) == 0)
    def _():
        for n, ref in enumerate(frames):
            stack_ref[n * CH : (n + 1) * CH] = ref[...]

    partial(h_ref[...], stack_ref, out_ref)


def filter_partial(place, hidden, frames, after=()):
    return call(
        filter_kernel,
        "filter_partial",
        place,
        [hidden] + frames,
        [PART],
        scratch=[pltpu.VMEM((STACK, CELLS), BF16)],
        steps=F_STEPS,
        in_specs=[pl.BlockSpec((ROWS // F_STEPS, CELLS), lambda i, *_: (i, 0))]
        + [whole((CH, CELLS))] * TAPS,
        out_specs=[pl.BlockSpec((PEERS * PER // F_STEPS, FLANES), lambda i, *_: (i, 0))],
        flops=2 * ROWS * STACK * CELLS,
        after=after,
        vmem=16,
    )[0]


def second_kernel(place_ref, w_at, active_at, *refs):
    pieces, frames, refs = refs[:CHANS], refs[CHANS : CHANS + TAPS], refs[CHANS + TAPS :]
    w_out, relu_out, out_ref, w_ref, h_ref, stack_ref, active_ref, sem = refs
    sources = [(w_at, w_ref), (active_at.at[0], active_ref)]
    copies = fetch(sem, sources + list(zip(pieces, stacked(h_ref, CHANS))) + list(zip(frames, stacked(stack_ref, TAPS))))
    for copy in copies:
        copy.wait()
    rows = PEERS * PER // F_STEPS
    for n in range(F_STEPS):
        hidden = arranged(True, n, place_ref, [h_ref[m * CH : (m + 1) * CH] for m in range(CHANS)])
        partial(hidden, stack_ref, out_ref.at[pl.ds(n * rows, rows)])
    relu_out[...] = jnp.maximum(active_ref[...], jnp.zeros((), BF16))
    turn_kernel(tuple(range(9)), place_ref, w_ref, w_out)


def second_work(place, w, active, pieces, frames, after):
    return call(
        second_kernel,
        "second_work",
        place,
        [w, active] + pieces + frames,
        [like((FULL, 9 * CH)), like((CH, CELLS))] + [PART],
        scratch=[
            pltpu.VMEM(w.shape, BF16),
            pltpu.VMEM((FULL, CELLS), BF16),
            pltpu.VMEM((STACK, CELLS), BF16),
            pltpu.VMEM((CH, CELLS), BF16),
            pltpu.SemaphoreType.DMA((2 + CHANS + TAPS,)),
        ],
        in_specs=[ANY] * (2 + CHANS + TAPS),
        vmem=26,
        after=after,
    )


def first_kernel(place_ref, t_at, s_at, t_out, s_out, t_ref, s_ref, sem):
    copies = fetch(sem, [(t_at, t_ref), (s_at, s_ref)])
    copies[0].wait()
    turn_kernel(ORDER, place_ref, t_ref, t_out)
    copies[1].wait()
    turn_kernel(tuple(range(9)), place_ref, s_ref, s_out)


def first_work(place, t, s, after):
    return call(
        first_kernel,
        "first_work",
        place,
        [t, s],
        [like((FULL, TAPS * CH)), like((FULL, 9 * CH))],
        scratch=[pltpu.VMEM(t.shape, BF16), pltpu.VMEM(s.shape, BF16), pltpu.SemaphoreType.DMA((2,))],
        in_specs=[ANY] * 2,
        vmem=22,
        after=after,
    )


def scatter(part, axis):
    part = lax.psum_scatter(part, axis, scatter_dimension=0, tiled=True)
    return part.reshape(-1, PER, FLANES)


def over_rest(part, axes):
    return lax.all_to_all(part, axes, 0, 0, tiled=True)


def filter_sum_kernel(factor, place_ref, in_ref, out_ref):
    total = jnp.sum(in_ref[...].astype(F32), axis=0) * factor
    for at, tap in enumerate(ORDER):
        out_ref[tap, 0:PER] = total[:, at * CH : (at + 1) * CH]
        start = LOW + (at % 4) * CH
        part = total[:, start : start + CH]
        out_ref[tap, PER:OWN] = part[0:4] if at < 4 else part[4:8]


def filter_sum(place, factor, x):
    return call(
        functools.partial(filter_sum_kernel, factor),
        "filter_sum",
        place,
        [x],
        [like((TAPS, OWN, CH), F32)],
    )[0]


def combine_kernel(place_ref, up_ref, keep_ref, got_ref, away_ref, out_ref):
    pair = (keep_ref[0].astype(F32) + got_ref[0].astype(F32)).astype(BF16).astype(F32)
    out_ref[...] = (up_ref[...].astype(F32) + pair + away_ref[...].astype(F32)).astype(BF16)


def combine(place, upstream, keep, got, away, after=()):
    flat = whole((CH, CELLS))
    own = pl.BlockSpec((1, CH, CELLS), lambda i, *_: (1, 0, 0))
    return call(
        combine_kernel,
        "combine",
        place,
        [upstream, keep, got, away],
        [like((CH, CELLS))],
        in_specs=[flat, own, own, flat],
        after=after,
    )[0]


def swap(x, axis):
    return lax.ppermute(x, axis, [(0, 1), (1, 0)])


def later(x):
    return lax.ppermute(x, SPACE, [(i + 1, i) for i in range(PEERS - 1)])


def earlier(x):
    return lax.ppermute(x, SPACE, [(i, i + 1) for i in range(PEERS - 1)])


def gather(hidden):
    far = swap(hidden, "xh")
    return [hidden, far, swap(hidden, "core"), swap(far, "core")]


def chan_sum(send, keep):
    got = swap(send, "core")
    pair = (keep[0].astype(F32) + got[0].astype(F32)).astype(BF16)
    return pair, (keep, got, swap(pair, "xh"))


def halo(x):
    down, up = [later(x)], [earlier(x)]
    for _ in range(2):
        down.append(later(down[-1]))
        up.append(earlier(up[-1]))
    return [down[1], down[0], x, up[0], up[1]], [down[2], up[2]]


def shards(cot, active_first, active_second, spatial_first, spatial_second, temporal_first, temporal_second):
    xh, core = lax.axis_index("xh"), lax.axis_index("core")
    chan = lambda a, b: a * 2 + b
    place = jnp.stack(
        [chan(1 - xh, 1 - core), chan(xh, 1 - core), chan(1 - xh, core), chan(xh, core)]
    ).astype(jnp.int32)
    factor = 1.0 / math.sqrt(PEERS * CELLS)
    nine = tuple(range(9))

    def pieces_of(hidden):
        own, far, near, cross = gather(hidden)
        return [cross, near, far, own]

    near, far = halo(cot[0])
    pieces = pieces_of(jnp.maximum(active_second[0], jnp.zeros((), BF16)))
    w_t = turn(place, temporal_second, ORDER)
    acc = temporal_near(place, w_t, near)
    pair, back = chan_sum(*temporal_far(place, w_t, acc, far, after=pieces[2:3]))
    w_s, hidden, part = second_work(
        place, spatial_second.reshape(9, CH, FULL), active_first, pieces, far + near, [pair]
    )
    pair, (keep, got, away) = chan_sum(*spatial(place, w_s, active_second, *back))
    part_second = scatter(tie([part], [pair])[0], "y")
    w_t, w_s = first_work(place, temporal_first, spatial_first.reshape(9, CH, FULL), [pair])
    middle = combine(place, cot[0], keep, got, away, after=[w_t])

    near, far = halo(middle)
    hidden = arrange(place, pieces_of(hidden))
    acc = temporal_near(place, w_t, near, after=[hidden])
    part = filter_partial(place, hidden, far + near, after=[acc])
    part_first = scatter(part, "z")
    pair, back = chan_sum(*temporal_far(place, w_t, acc, far, after=[part]))
    pair, (keep, got, away) = chan_sum(*spatial(place, w_s, active_first, *back))
    own = (keep[1].astype(F32) + got[1].astype(F32)).astype(BF16).astype(F32)
    result = (middle.astype(F32) + own + away.astype(F32)).astype(BF16)

    part_second = over_rest(tie([part_second], [away])[0], ("z", "xl"))
    part_first = over_rest(tie([part_first], [away, part_second])[0], ("y", "xl"))
    filter_first = filter_sum(place, factor, part_first)
    filter_second = filter_sum(place, factor, part_second)
    return result[None], filter_first, filter_second


def solution(mesh):
    fine = Mesh(mesh.devices.reshape(4, 2, 8, 2, 2), SPACE + ("xh", "core"))
    chan = ("xh", "core")
    return jax.shard_map(
        shards,
        mesh=fine,
        in_specs=(
            P(SPACE, chan, None),
            P(SPACE, chan, None),
            P(SPACE, chan, None),
            P(None, None, chan, None),
            P(None, None, chan, None),
            P(None, chan, None),
            P(None, chan, None),
        ),
        out_specs=(P(SPACE, chan, None), P(None, SPACE, chan), P(None, SPACE, chan)),
        check_vma=False,
    )
```

```python
import functools
import math

import jax
import jax.numpy as jnp
from jax import lax
from jax.experimental import pallas as pl
from jax.experimental.pallas import tpu as pltpu
from jax.sharding import Mesh
from jax.sharding import PartitionSpec as P

TAPS = 7
HGT = 16
WID = 28
CLIPS = 2
PEERS = 64
CH = 192
CHANS = 4
FULL = CH * CHANS
CELLS = CLIPS * HGT * WID
OWN = FULL // PEERS
PER = 8
ORDER = (0, 6, 1, 2, 3, 4, 5)
FAR = 2 * CH
STACK = TAPS * CH
LOW = 1408
FLANES = LOW + 4 * CH
SPACE = ("y", "xl", "z")
F32 = jnp.float32
BF16 = jnp.bfloat16
NT = (((1,), (1,)), ((), ()))
MIB = 1024 * 1024


ANY = pl.BlockSpec(memory_space=pl.ANY)


def fetch(sem, pairs):
    copies = [pltpu.make_async_copy(a, b, sem.at[n]) for n, (a, b) in enumerate(pairs)]
    for copy in copies:
        copy.start()
    return copies


def stacked(ref, count):
    return [ref.at[pl.ds(n * CH, CH)] for n in range(count)]


def cost(flops, moved):
    return pl.CostEstimate(flops=int(flops) // 64, bytes_accessed=int(moved) // 64, transcendentals=0)


def whole(shape):
    return pl.BlockSpec(shape, lambda i, *_: (0,) * len(shape))


def call(kernel, name, scalars, ins, outs, scratch=(), steps=1, vmem=10, in_specs=None, out_specs=None, flops=0, after=()):
    moved = sum(math.prod(x.shape) * x.dtype.itemsize for x in list(ins) + list(outs))
    n, m = 1 + len(ins), len(after)

    def body(*refs):
        kernel(*refs[:n], *refs[n + m :])

    return pl.pallas_call(
        body,
        grid_spec=pltpu.PrefetchScalarGridSpec(
            num_scalar_prefetch=1,
            grid=(steps,),
            in_specs=(in_specs or [whole(x.shape) for x in ins]) + [ANY] * m,
            out_specs=out_specs or [whole(x.shape) for x in outs],
            scratch_shapes=list(scratch),
        ),
        out_shape=list(outs),
        compiler_params=pltpu.CompilerParams(vmem_limit_bytes=vmem * MIB),
        cost_estimate=cost(flops, moved),
        name=name,
    )(scalars, *ins, *after)


def tie(arrays, after):
    count, m = len(arrays), len(after)

    def body(*refs):
        pass

    anywhere = pl.BlockSpec(memory_space=pl.ANY)
    return pl.pallas_call(
        body,
        in_specs=[anywhere] * (count + m),
        out_specs=[anywhere] * count,
        out_shape=[like(x.shape, x.dtype) for x in arrays],
        input_output_aliases={i: i for i in range(count)},
        name="tie",
    )(*arrays, *after)


def like(shape, dtype=BF16):
    return jax.ShapeDtypeStruct(shape, dtype)


def turn_kernel(taps, place_ref, w_ref, out_ref):
    row = lax.broadcasted_iota(jnp.int32, (FULL, 1), 0)
    want = row + (place_ref[0]) * CH
    for slot in range(1, CHANS):
        want = jnp.where(row >= slot * CH, row + (place_ref[slot] - slot) * CH, want)
    lane = lax.broadcasted_iota(jnp.int32, (FULL, FULL), 1)
    pick = jnp.where(lane == want, 1.0, 0.0).astype(BF16)
    for n in range(0, len(taps), 2):
        pair = [lax.dot_general(pick, w_ref[tap], NT, preferred_element_type=F32) for tap in taps[n : n + 2]]
        pair = pair[0] if len(pair) == 1 else jnp.concatenate(pair, axis=1)
        out_ref[:, n * CH : n * CH + pair.shape[1]] = pair.astype(BF16)


def turn(place, w, taps, after=()):
    return call(
        functools.partial(turn_kernel, taps),
        "turn",
        place,
        [w],
        [like((FULL, len(taps) * CH))],
        flops=2 * FULL * FULL * CH * len(taps),
        after=after,
        vmem=16,
    )[0]


def arranged(along_y, step, place_ref, pieces):
    half = PEERS // F_STEPS * PER
    row = lax.broadcasted_iota(jnp.int32, (2 * half, 1), 0)
    low = row < half
    at = jnp.where(low, row, row - half)
    spot = lax.shift_right_logical(at, 3)
    if along_y:
        peer = step * 16 + spot
    else:
        peer = lax.bitwise_and(spot, 7) * 8 + step * 2 + lax.shift_right_logical(spot, 3)
    inner = jnp.where(low, lax.bitwise_and(at, 7), 8 + lax.bitwise_and(at, 3))
    want = peer * OWN + inner
    lane = lax.broadcasted_iota(jnp.int32, (2 * half, CH), 1)
    total = None
    for slot, piece in enumerate(pieces):
        pick = jnp.where(lane + place_ref[slot] * CH == want, 1.0, 0.0).astype(BF16)
        t = jnp.dot(pick, piece, preferred_element_type=F32)
        total = t if total is None else total + t
    return total.astype(BF16)


def arrange_kernel(place_ref, a_ref, b_ref, c_ref, d_ref, out_ref):
    pieces = [ref[...] for ref in (a_ref, b_ref, c_ref, d_ref)]
    out_ref[...] = arranged(False, pl.program_id(0), place_ref, pieces)


F_STEPS = 4
ROWS = 2 * PEERS * PER


def arrange(place, pieces, after=()):
    return call(
        arrange_kernel,
        "arrange",
        place,
        pieces,
        [like((ROWS, CELLS))],
        steps=F_STEPS,
        out_specs=[pl.BlockSpec((ROWS // F_STEPS, CELLS), lambda i, *_: (i, 0))],
        flops=2 * ROWS * FULL * CELLS,
        after=after,
    )[0]


def near_kernel(place_ref, w_ref, a_ref, b_ref, c_ref, d_ref, e_ref, out_ref, stack_ref):
    step = pl.program_id(0)

    @pl.when(step == 0)
    def _():
        for n, ref in enumerate((a_ref, b_ref, c_ref, d_ref, e_ref)):
            stack_ref[n * CH : (n + 1) * CH] = ref[...]

    out_ref[...] = jnp.dot(w_ref[:, FAR:], stack_ref[...], preferred_element_type=F32)


T_STEPS = 4


def temporal_near(place, w, frames, after=()):
    rows = FULL // T_STEPS
    return call(
        near_kernel,
        "temporal_near",
        place,
        [w] + frames,
        [like((FULL, CELLS), F32)],
        scratch=[pltpu.VMEM((5 * CH, CELLS), BF16)],
        steps=T_STEPS,
        in_specs=[pl.BlockSpec((rows, STACK), lambda i, *_: (i, 0))] + [whole((CH, CELLS))] * 5,
        out_specs=[pl.BlockSpec((rows, CELLS), lambda i, *_: (i, 0))],
        flops=2 * FULL * 5 * CH * CELLS,
        after=after,
    )[0]


def far_kernel(place_ref, w_ref, acc_ref, a_ref, b_ref, send_ref, keep_ref, stack_ref):
    step = pl.program_id(0)

    @pl.when(step == 0)
    def _():
        stack_ref[0:CH] = a_ref[...]
        stack_ref[CH:] = b_ref[...]

    v = acc_ref[...] + jnp.dot(w_ref[:, :FAR], stack_ref[...], preferred_element_type=F32)
    v = v.astype(BF16)
    for n in range(CHANS):

        @pl.when(step == n)
        def _():
            (send_ref if n < 2 else keep_ref)[n % 2] = v


def temporal_far(place, w, acc, frames, after=()):
    return call(
        far_kernel,
        "temporal_far",
        place,
        [w, acc] + frames,
        [like((2, CH, CELLS))] * 2,
        scratch=[pltpu.VMEM((FAR, CELLS), BF16)],
        steps=CHANS,
        in_specs=[
            pl.BlockSpec((CH, STACK), lambda i, *_: (i, 0)),
            pl.BlockSpec((CH, CELLS), lambda i, *_: (i, 0)),
        ]
        + [whole((CH, CELLS))] * 2,
        flops=2 * FULL * FAR * CELLS,
        after=after,
    )


def spatial_kernel(place_ref, w_ref, active_ref, keep_ref, got_ref, far_ref, send_ref, out_ref, win_ref):
    step = pl.program_id(0)

    @pl.when(step == 0)
    def _():
        pair = (keep_ref[1].astype(F32) + got_ref[1].astype(F32)).astype(BF16).astype(F32)
        back = (pair + far_ref[...].astype(F32)).astype(BF16).astype(F32)
        masked = jnp.where(active_ref[0].astype(F32) > 0, back, 0.0)
        cell = lax.broadcasted_iota(jnp.int32, (1, CELLS), 1)
        cell = jnp.where(cell < HGT * WID, cell, cell - HGT * WID)
        line = lax.shift_right_logical(cell * 2341, 16)
        spot = cell - line * WID
        for row in range(3):
            for col in range(3):
                down, right = 1 - row, 1 - col
                shift = down * WID + right
                v = masked if shift == 0 else pltpu.roll(masked, (-shift) % CELLS, 1)
                if shift != 0:
                    ok = (line + down >= 0) & (line + down < HGT)
                    ok = ok & (spot + right >= 0) & (spot + right < WID)
                    v = jnp.where(ok, v, 0.0)
                n = row * 3 + col
                win_ref[n * CH : (n + 1) * CH] = v.astype(BF16)

    v = jnp.dot(w_ref[...], win_ref[...], preferred_element_type=F32).astype(BF16)
    for n in range(CHANS):

        @pl.when(step == n)
        def _():
            (send_ref if n < 2 else out_ref)[n % 2] = v


def spatial(place, w, active, keep, got, far, after=()):
    return call(
        spatial_kernel,
        "spatial",
        place,
        [w, active, keep, got, far],
        [like((2, CH, CELLS))] * 2,
        scratch=[pltpu.VMEM((9 * CH, CELLS), BF16)],
        steps=CHANS,
        in_specs=[pl.BlockSpec((CH, 9 * CH), lambda i, *_: (i, 0))]
        + [whole(x.shape) for x in (active, keep, got, far)],
        flops=2 * FULL * 9 * CH * CELLS,
        after=after,
        vmem=18,
    )


def partial(hidden, stack_ref, out_ref):
    acc = lax.dot_general(hidden, stack_ref[...], NT, preferred_element_type=F32)
    half = PEERS // F_STEPS * PER
    low, rest = acc[:half], acc[half:]
    out_ref[:, 0:LOW] = jnp.concatenate([low, jnp.zeros((half, LOW - STACK), F32)], axis=1).astype(BF16)
    upper = lax.bitwise_and(lax.broadcasted_iota(jnp.int32, (half, 4 * CH), 0), 7) < 4
    wide = jnp.concatenate([rest[:, 4 * CH :], jnp.zeros((half, CH), F32)], axis=1)
    out_ref[:, LOW:] = jnp.where(upper, rest[:, : 4 * CH], wide).astype(BF16)


PART = like((PEERS * PER, FLANES))


def filter_kernel(place_ref, h_ref, *refs):
    frames, (out_ref, stack_ref) = refs[:TAPS], refs[TAPS:]

    @pl.when(pl.program_id(0) == 0)
    def _():
        for n, ref in enumerate(frames):
            stack_ref[n * CH : (n + 1) * CH] = ref[...]

    partial(h_ref[...], stack_ref, out_ref)


def filter_partial(place, hidden, frames, after=()):
    return call(
        filter_kernel,
        "filter_partial",
        place,
        [hidden] + frames,
        [PART],
        scratch=[pltpu.VMEM((STACK, CELLS), BF16)],
        steps=F_STEPS,
        in_specs=[pl.BlockSpec((ROWS // F_STEPS, CELLS), lambda i, *_: (i, 0))]
        + [whole((CH, CELLS))] * TAPS,
        out_specs=[pl.BlockSpec((PEERS * PER // F_STEPS, FLANES), lambda i, *_: (i, 0))],
        flops=2 * ROWS * STACK * CELLS,
        after=after,
        vmem=16,
    )[0]


def second_kernel(place_ref, w_at, active_at, *refs):
    pieces, frames, refs = refs[:CHANS], refs[CHANS : CHANS + TAPS], refs[CHANS + TAPS :]
    w_out, relu_out, out_ref, w_ref, h_ref, stack_ref, active_ref, sem = refs
    sources = [(w_at, w_ref), (active_at.at[0], active_ref)]
    copies = fetch(sem, sources + list(zip(pieces, stacked(h_ref, CHANS))) + list(zip(frames, stacked(stack_ref, TAPS))))
    for copy in copies:
        copy.wait()
    rows = PEERS * PER // F_STEPS
    for n in range(F_STEPS):
        hidden = arranged(True, n, place_ref, [h_ref[m * CH : (m + 1) * CH] for m in range(CHANS)])
        partial(hidden, stack_ref, out_ref.at[pl.ds(n * rows, rows)])
    relu_out[...] = jnp.maximum(active_ref[...], jnp.zeros((), BF16))
    turn_kernel(tuple(range(9)), place_ref, w_ref, w_out)


def second_work(place, w, active, pieces, frames, after):
    return call(
        second_kernel,
        "second_work",
        place,
        [w, active] + pieces + frames,
        [like((FULL, 9 * CH)), like((CH, CELLS))] + [PART],
        scratch=[
            pltpu.VMEM(w.shape, BF16),
            pltpu.VMEM((FULL, CELLS), BF16),
            pltpu.VMEM((STACK, CELLS), BF16),
            pltpu.VMEM((CH, CELLS), BF16),
            pltpu.SemaphoreType.DMA((2 + CHANS + TAPS,)),
        ],
        in_specs=[ANY] * (2 + CHANS + TAPS),
        vmem=26,
        after=after,
    )


def first_kernel(place_ref, t_at, s_at, t_out, s_out, t_ref, s_ref, sem):
    copies = fetch(sem, [(t_at, t_ref), (s_at, s_ref)])
    copies[0].wait()
    turn_kernel(ORDER, place_ref, t_ref, t_out)
    copies[1].wait()
    turn_kernel(tuple(range(9)), place_ref, s_ref, s_out)


def first_work(place, t, s, after):
    return call(
        first_kernel,
        "first_work",
        place,
        [t, s],
        [like((FULL, TAPS * CH)), like((FULL, 9 * CH))],
        scratch=[pltpu.VMEM(t.shape, BF16), pltpu.VMEM(s.shape, BF16), pltpu.SemaphoreType.DMA((2,))],
        in_specs=[ANY] * 2,
        vmem=22,
        after=after,
    )


def scatter(part, axis):
    part = lax.psum_scatter(part, axis, scatter_dimension=0, tiled=True)
    return part.reshape(-1, PER, FLANES)


def over_rest(part, axes):
    return lax.all_to_all(part, axes, 0, 0, tiled=True)


def filter_sum_kernel(factor, place_ref, in_ref, out_ref):
    total = jnp.sum(in_ref[...].astype(F32), axis=0) * factor
    for at, tap in enumerate(ORDER):
        out_ref[tap, 0:PER] = total[:, at * CH : (at + 1) * CH]
        start = LOW + (at % 4) * CH
        part = total[:, start : start + CH]
        out_ref[tap, PER:OWN] = part[0:4] if at < 4 else part[4:8]


def filter_sum(place, factor, x):
    return call(
        functools.partial(filter_sum_kernel, factor),
        "filter_sum",
        place,
        [x],
        [like((TAPS, OWN, CH), F32)],
    )[0]


def combine_kernel(place_ref, up_ref, keep_ref, got_ref, away_ref, out_ref):
    pair = (keep_ref[0].astype(F32) + got_ref[0].astype(F32)).astype(BF16).astype(F32)
    out_ref[...] = (up_ref[...].astype(F32) + pair + away_ref[...].astype(F32)).astype(BF16)


def combine(place, upstream, keep, got, away, after=()):
    flat = whole((CH, CELLS))
    own = pl.BlockSpec((1, CH, CELLS), lambda i, *_: (1, 0, 0))
    return call(
        combine_kernel,
        "combine",
        place,
        [upstream, keep, got, away],
        [like((CH, CELLS))],
        in_specs=[flat, own, own, flat],
        after=after,
    )[0]


def swap(x, axis):
    return lax.ppermute(x, axis, [(0, 1), (1, 0)])


def later(x):
    return lax.ppermute(x, SPACE, [(i + 1, i) for i in range(PEERS - 1)])


def earlier(x):
    return lax.ppermute(x, SPACE, [(i, i + 1) for i in range(PEERS - 1)])


def gather(hidden):
    far = swap(hidden, "xh")
    return [hidden, far, swap(hidden, "core"), swap(far, "core")]


def chan_sum(send, keep):
    got = swap(send, "core")
    pair = (keep[0].astype(F32) + got[0].astype(F32)).astype(BF16)
    return pair, (keep, got, swap(pair, "xh"))


def halo(x):
    down, up = [later(x)], [earlier(x)]
    for _ in range(2):
        down.append(later(down[-1]))
        up.append(earlier(up[-1]))
    return [down[1], down[0], x, up[0], up[1]], [down[2], up[2]]


def shards(cot, active_first, active_second, spatial_first, spatial_second, temporal_first, temporal_second):
    xh, core = lax.axis_index("xh"), lax.axis_index("core")
    chan = lambda a, b: a * 2 + b
    place = jnp.stack(
        [chan(1 - xh, 1 - core), chan(xh, 1 - core), chan(1 - xh, core), chan(xh, core)]
    ).astype(jnp.int32)
    factor = 1.0 / math.sqrt(PEERS * CELLS)
    nine = tuple(range(9))

    def pieces_of(hidden):
        own, far, near, cross = gather(hidden)
        return [cross, near, far, own]

    near, far = halo(cot[0])
    pieces = pieces_of(jnp.maximum(active_second[0], jnp.zeros((), BF16)))
    w_t = turn(place, temporal_second, ORDER)
    acc = temporal_near(place, w_t, near)
    pair, back = chan_sum(*temporal_far(place, w_t, acc, far, after=pieces[2:3]))
    w_s, hidden, part = second_work(
        place, spatial_second.reshape(9, CH, FULL), active_first, pieces, far + near, [pair]
    )
    pair, (keep, got, away) = chan_sum(*spatial(place, w_s, active_second, *back))
    part_second = scatter(tie([part], [pair])[0], ("y", "xl"))
    w_t, w_s = first_work(place, temporal_first, spatial_first.reshape(9, CH, FULL), [pair])
    middle = combine(place, cot[0], keep, got, away, after=[w_t])

    near, far = halo(middle)
    hidden = arrange(place, pieces_of(hidden))
    acc = temporal_near(place, w_t, near, after=[hidden])
    part = filter_partial(place, hidden, far + near, after=[acc])
    part_first = scatter(part, "z")
    pair, back = chan_sum(*temporal_far(place, w_t, acc, far, after=[part]))
    pair, (keep, got, away) = chan_sum(*spatial(place, w_s, active_first, *back))
    own = (keep[1].astype(F32) + got[1].astype(F32)).astype(BF16).astype(F32)
    result = (middle.astype(F32) + own + away.astype(F32)).astype(BF16)

    part_second = over_rest(tie([part_second], [away])[0], "z")
    part_first = over_rest(tie([part_first], [away, part_second])[0], ("y", "xl"))
    filter_first = filter_sum(place, factor, part_first)
    filter_second = filter_sum(place, factor, part_second)
    return result[None], filter_first, filter_second


def solution(mesh):
    fine = Mesh(mesh.devices.reshape(4, 2, 8, 2, 2), SPACE + ("xh", "core"))
    chan = ("xh", "core")
    return jax.shard_map(
        shards,
        mesh=fine,
        in_specs=(
            P(SPACE, chan, None),
            P(SPACE, chan, None),
            P(SPACE, chan, None),
            P(None, None, chan, None),
            P(None, None, chan, None),
            P(None, chan, None),
            P(None, chan, None),
        ),
        out_specs=(P(SPACE, chan, None), P(None, SPACE, chan), P(None, SPACE, chan)),
        check_vma=False,
    )
```
